256 devices in a mesh: ens: 2 (over x_hi), row: 32 (over z, y), col: 4 (over x_lo, core).
Axes of the slice: x: 4 (x_hi: 2, x_lo: 2; x = x_hi * 2 + x_lo), y: 4, z: 8, core: 2. Of those that a mesh axis runs over, the one named last changes fastest.
Arguments:
- adjoint: float32 [2, 3, 8, 512, 2048], P('ens', None, 'col', 'row'), may hold values from -6 to 6
- base_flow: float32 [2, 2, 8, 512, 2048], P('ens', None, 'col', 'row'), may hold values from -6 to 6
- stream_first: float32 [16, 128, 128], replicated, may hold values from -0.125 to 0.125
- stream_second: float32 [16, 128, 128], replicated, may hold values from -0.125 to 0.125
- wall_first: float32 [512, 512], replicated, may hold values from -0.25 to 0.25
- wall_second: float32 [512, 512], replicated, may hold values from -0.25 to 0.25
- forcing: float32 [3, 8, 512, 2048], P(None, 'col', 'row'), may hold values from 0.3 to 3
Outputs:
- updated: float32 [2, 3, 8, 512, 2048], P('ens', None, 'col', 'row')
- gradient: float32 [3, 8, 512, 2048], P(None, 'col', 'row')
The draws below stay inside these ranges and needn't reach their ends.
All inputs are finite; a program needn't handle non-finite values.
Results may differ from the reference program's by a relative error of at most 0.000071.
Values sent between devices are 32-bit elements; how exact they have to be, the bound alone decides.
No kernel may reach another device: no remote copies, remote signals or barrier semaphores. Data moves between devices by JAX's collectives and lax.ppermute only.
A program may use at most 128 MiB of HBM per device.

```python
import math
import jax
import jax.numpy as jnp
from jax import lax

NX = 2048
NY = 512
BLK = 128
NBX = 16
NZ = 8
MEMBERS = 2


def block_levels(rng, shape, cuts, smallest, largest):
    factor_of = 1.0
    for dim, shards_of in cuts:
        draws = jax.random.uniform(jax.random.fold_in(jax.random.fold_in(rng, 6), dim), (shards_of,), jnp.float32, smallest / len(cuts), largest / len(cuts))
        factor_of = factor_of * jnp.repeat(jnp.exp(draws), shape[dim] // shards_of).reshape((-1,) + (1,) * (len(shape) - 1 - dim))
    return factor_of


def bell_draw(own_key, dims, scale, most, cuts=(), held_as=jnp.bfloat16):
    values = scale * jax.random.normal(own_key, dims, jnp.float32)
    if cuts:
        values = values * block_levels(own_key, dims, cuts, -0.22, 0.18)
    return jnp.clip(values, -most, most).astype(held_as)


def setup_inputs(seed: int = 0) -> dict:
    key_of = jax.random.split(jax.random.key(seed), 8)
    adjoint = bell_draw(key_of[0], (MEMBERS, 3, NZ, NY, NX), 1.0, 6.0, ((0, 2), (2, 4), (3, 32)), jnp.float32)
    base_flow = bell_draw(key_of[1], (MEMBERS, 2, NZ, NY, NX), 1.0, 6.0, ((0, 2), (2, 4), (3, 32)), jnp.float32)
    stream_first = bell_draw(key_of[2], (NBX, BLK, BLK), NX ** -0.5, 0.125, (), jnp.float32)
    stream_second = bell_draw(key_of[3], (NBX, BLK, BLK), NX ** -0.5, 0.125, (), jnp.float32)
    wall_first = bell_draw(key_of[4], (NY, NY), NY ** -0.5, 0.25, (), jnp.float32)
    wall_second = bell_draw(key_of[5], (NY, NY), NY ** -0.5, 0.25, (), jnp.float32)
    forcing = jnp.clip(jnp.exp(math.log(3.0) - 2.3025851 * jax.random.uniform(key_of[6], (3, NZ, NY, NX), jnp.float32) ** block_levels(key_of[6], (3, NZ, NY, NX), ((1, 4), (2, 32)), -0.2, 0.2)), 0.3, 3.0)
    return {"adjoint": adjoint, "base_flow": base_flow, "stream_first": stream_first, "stream_second": stream_second, "wall_first": wall_first, "wall_second": wall_second, "forcing": forcing}


viscosity = 0.5
step_weight = 0.25


def circulant(blocks):
    block_count = blocks.shape[0]
    block_size = blocks.shape[1]
    rows_index = jnp.arange(block_count, dtype=jnp.int32)
    offsets = ((rows_index[None, :] - rows_index[:, None]) % block_count).astype(jnp.int32)
    tiled = blocks[offsets]
    return tiled.transpose(0, 2, 1, 3).reshape(block_count * block_size, block_count * block_size)


def along_stream(values, operator):
    return jnp.einsum('...j,ij->...i', values, operator, precision=lax.Precision.HIGHEST)


def along_wall(values, operator):
    return jnp.einsum('ky,...yx->...kx', operator, values, precision=lax.Precision.HIGHEST)


def reference(adjoint, base_flow, stream_first, stream_second, wall_first, wall_second, forcing):
    dense_first = circulant(stream_first)
    dense_second = circulant(stream_second)

    def member(pair):
        adj_field, base_speed = pair
        x_first = along_stream(adj_field, dense_first)
        x_second = along_stream(adj_field, dense_second)
        rhs_stream = viscosity * x_second + base_speed[0:1] * x_first
        y_first = along_wall(adj_field, wall_first)
        y_second = along_wall(adj_field, wall_second)
        rhs_wall = viscosity * y_second + base_speed[1:2] * y_first
        return adj_field + step_weight * (rhs_stream + rhs_wall)

    updated = lax.map(member, (adjoint, base_flow))
    gradient = forcing * jnp.sum(updated, axis=0)
    return updated, gradient
```

```python
import functools

import jax
import jax.numpy as jnp
from jax import lax
from jax.experimental import pallas as pl
from jax.experimental.pallas import tpu as pltpu
from jax.sharding import PartitionSpec as P

viscosity = 0.5
step_weight = 0.25
LANE = 128


def halves(value):
    high = value.astype(jnp.bfloat16)
    low = (value - high.astype(jnp.float32)).astype(jnp.bfloat16)
    return high, low


def product(left, right, contract):
    dims = ((contract[0:1], contract[1:2]), ((), ()))
    dot = functools.partial(
        lax.dot_general, dimension_numbers=dims, preferred_element_type=jnp.float32
    )
    return dot(left[0], right[0]) + (dot(left[0], right[1]) + dot(left[1], right[0]))


def pack_kernel(adj_ref, base_ref, out_ref):
    fields = adj_ref.shape[1]
    for chunk in range(out_ref.shape[0]):
        lanes = pl.ds(chunk * LANE, LANE)
        for field in range(fields):
            out_ref[chunk, field] = adj_ref[0, field, 0, :, lanes]
        out_ref[chunk, fields] = base_ref[0, 0, 0, :, lanes]


def pack(adjoint, base_flow):
    _, fields, planes, rows, nx = adjoint.shape
    chunks = nx // LANE
    return pl.pallas_call(
        pack_kernel,
        grid=(planes,),
        in_specs=[
            pl.BlockSpec((1, fields, 1, rows, nx), lambda z: (0, 0, z, 0, 0)),
            pl.BlockSpec((1, 1, 1, rows, nx), lambda z: (0, 1, z, 0, 0)),
        ],
        out_specs=pl.BlockSpec((chunks, fields + 1, rows, LANE), lambda z: (z, 0, 0, 0)),
        out_shape=jax.ShapeDtypeStruct((planes * chunks, fields + 1, rows, LANE), jnp.float32),
        name="pack_lines",
    )(adjoint, base_flow)


def stream_kernel(
    adj_ref, base_ref, first_ref, second_ref, wall1_ref, wall2_ref,
    out_ref, whigh_ref, wlow_ref, high_ref, low_ref, acc_ref,
):
    step = pl.program_id(0)
    _, fields, planes, rows, nx = adj_ref.shape
    blocks = nx // LANE
    lines = fields * planes * rows

    for which, ref in enumerate((wall1_ref, wall2_ref)):
        whigh_ref[which], wlow_ref[which] = halves(ref[...])

    @pl.when(step == 0)
    def _():
        for q in range(blocks):
            block = adj_ref[0, :, :, :, pl.ds(q * LANE, LANE)].reshape(lines, LANE)
            high, low = halves(block)
            for place in (q, q + blocks):
                if place < 2 * blocks - 1:
                    high_ref[pl.ds(place * lines, lines), :] = high
                    low_ref[pl.ds(place * lines, lines), :] = low
        acc_ref[...] = jnp.zeros_like(acc_ref)

    weights = jnp.concatenate(
        [
            jnp.concatenate([first_ref[0], first_ref[1]], axis=1),
            jnp.concatenate([second_ref[0], second_ref[1]], axis=1),
        ],
        axis=0,
    )
    total = blocks * lines
    near = pl.ds(pl.multiple_of(step * (2 * lines), 2 * lines), total)
    far = pl.ds(pl.multiple_of(step * (2 * lines) + lines, lines), total)
    left = tuple(
        jnp.concatenate([ref[near, :], ref[far, :]], axis=1) for ref in (high_ref, low_ref)
    )
    acc_ref[...] += product(left, halves(weights), (1, 1))

    @pl.when(step == pl.num_programs(0) - 1)
    def _():
        for p in range(blocks):
            lanes = pl.ds(p * LANE, LANE)
            x_first = acc_ref[pl.ds(p * lines, lines), pl.ds(0, LANE)]
            x_second = acc_ref[pl.ds(p * lines, lines), pl.ds(LANE, LANE)]
            x_first = x_first.reshape(fields, planes, rows, LANE)
            x_second = x_second.reshape(fields, planes, rows, LANE)
            rhs = viscosity * x_second + base_ref[0, 0, :, :, lanes][None] * x_first
            out_ref[:, :, :, lanes] = adj_ref[0, :, :, :, lanes] + step_weight * rhs


def stream(adjoint, base_flow, stream_first, stream_second, wall_first, wall_second):
    _, fields, planes, rows, nx = adjoint.shape
    blocks = nx // LANE
    lines = fields * planes * rows
    steps = blocks // 2
    ny = wall_first.shape[0]
    wall_rows = ny // steps
    whole = lambda i: (0, 0, 0, 0, 0)
    return pl.pallas_call(
        stream_kernel,
        grid=(steps,),
        in_specs=[
            pl.BlockSpec((1, fields, planes, rows, nx), whole),
            pl.BlockSpec((1, 1, planes, rows, nx), whole),
            pl.BlockSpec((2, LANE, LANE), lambda i: (i, 0, 0)),
            pl.BlockSpec((2, LANE, LANE), lambda i: (i, 0, 0)),
            pl.BlockSpec((wall_rows, ny), lambda i: (i, 0)),
            pl.BlockSpec((wall_rows, ny), lambda i: (i, 0)),
        ],
        out_specs=[
            pl.BlockSpec((fields, planes, rows, nx), lambda i: (0, 0, 0, 0)),
            pl.BlockSpec((2, wall_rows, ny), lambda i: (0, i, 0)),
            pl.BlockSpec((2, wall_rows, ny), lambda i: (0, i, 0)),
        ],
        out_shape=[
            jax.ShapeDtypeStruct((fields, planes, rows, nx), jnp.float32),
            jax.ShapeDtypeStruct((2, ny, ny), jnp.bfloat16),
            jax.ShapeDtypeStruct((2, ny, ny), jnp.bfloat16),
        ],
        scratch_shapes=[
            pltpu.VMEM(((2 * blocks - 1) * lines, LANE), jnp.bfloat16),
            pltpu.VMEM(((2 * blocks - 1) * lines, LANE), jnp.bfloat16),
            pltpu.VMEM((blocks * lines, 2 * LANE), jnp.float32),
        ],
        compiler_params=pltpu.CompilerParams(vmem_limit_bytes=32 * 2**20),
        cost_estimate=pl.CostEstimate(
            flops=6 * 2 * lines * nx * nx, bytes_accessed=8 * 2**20, transcendentals=0
        ),
        name="stream_sweep",
    )(adjoint, base_flow, stream_first, stream_second, wall_first, wall_second)


def wall_kernel(lines_ref, whigh_ref, wlow_ref, out_ref):
    chunks, slabs, rows, _ = lines_ref.shape
    fields = slabs - 1
    ny = chunks * rows
    parts = [halves(lines_ref[:, f].reshape(ny, LANE)) for f in range(fields)]
    values = tuple(jnp.concatenate([part[k] for part in parts], axis=1) for k in range(2))
    y_first = product((whigh_ref[0], wlow_ref[0]), values, (1, 0))
    y_second = product((whigh_ref[1], wlow_ref[1]), values, (1, 0))
    speed = lines_ref[:, fields].reshape(ny, LANE)
    for f in range(fields):
        lanes = slice(f * LANE, (f + 1) * LANE)
        rhs = step_weight * (viscosity * y_second[:, lanes] + speed * y_first[:, lanes])
        out_ref[:, f] = rhs.reshape(chunks, rows, LANE)


def wall(lines, whigh, wlow):
    chunks, slabs, rows, _ = lines.shape
    ny = chunks * rows
    return pl.pallas_call(
        wall_kernel,
        out_shape=jax.ShapeDtypeStruct((chunks, slabs - 1, rows, LANE), jnp.float32),
        compiler_params=pltpu.CompilerParams(vmem_limit_bytes=32 * 2**20),
        cost_estimate=pl.CostEstimate(
            flops=6 * 2 * ny * ny * LANE * (slabs - 1), bytes_accessed=4 * 2**20, transcendentals=0
        ),
        name="wall_sweep",
    )(lines, whigh, wlow)


def update_kernel(stream_ref, wall_ref, out_ref):
    for chunk in range(wall_ref.shape[0]):
        lanes = pl.ds(chunk * LANE, LANE)
        out_ref[0, :, 0, :, lanes] = stream_ref[:, 0, :, lanes] + wall_ref[chunk]


def gradient_kernel(updated_ref, stream_ref, wall_ref, forcing_ref, out_ref):
    for chunk in range(wall_ref.shape[0]):
        lanes = pl.ds(chunk * LANE, LANE)
        other = stream_ref[:, 0, :, lanes] + wall_ref[chunk]
        out_ref[:, 0, :, lanes] = forcing_ref[:, 0, :, lanes] * (
            updated_ref[0, :, 0, :, lanes] + other
        )


def pencil_specs(fields, planes, rows, nx, parts):
    width = nx // parts
    held = pl.BlockSpec((fields, 1, rows, width), lambda z, h: (0, z, 0, h))
    member = pl.BlockSpec((1, fields, 1, rows, width), lambda z, h: (0, 0, z, 0, h))
    slabs = pl.BlockSpec((width // LANE, fields, rows, LANE), lambda z, h: (z * parts + h, 0, 0, 0))
    return held, member, slabs


def update(streamed, walled):
    fields, planes, rows, nx = streamed.shape
    parts = 2
    held, member, slabs = pencil_specs(fields, planes, rows, nx, parts)
    return pl.pallas_call(
        update_kernel,
        grid=(planes, parts),
        in_specs=[held, slabs],
        out_specs=member,
        out_shape=jax.ShapeDtypeStruct((1, fields, planes, rows, nx), jnp.float32),
        name="add_sweeps",
    )(streamed, walled)


def gradient(updated, streamed, walled, forcing):
    fields, planes, rows, nx = streamed.shape
    parts = 2
    held, member, slabs = pencil_specs(fields, planes, rows, nx, parts)
    return pl.pallas_call(
        gradient_kernel,
        grid=(planes, parts),
        in_specs=[member, held, slabs, held],
        out_specs=held,
        out_shape=jax.ShapeDtypeStruct((fields, planes, rows, nx), jnp.float32),
        name="body_force",
    )(updated, streamed, walled, forcing)


def local(adjoint, base_flow, stream_first, stream_second, wall_first, wall_second, forcing):
    swap = [(0, 1), (1, 0)]
    lines = lax.all_to_all(pack(adjoint, base_flow), "row", 0, 0)
    streamed, whigh, wlow = stream(
        adjoint, base_flow, stream_first, stream_second, wall_first, wall_second
    )
    other_streamed = lax.ppermute(streamed, "ens", swap)
    walled = lax.all_to_all(wall(lines, whigh, wlow), "row", 0, 0)
    other_walled = lax.ppermute(walled, "ens", swap)
    updated = update(streamed, walled)
    return updated, gradient(updated, other_streamed, other_walled, forcing)


def solution(mesh):
    placed = (
        P("ens", None, "col", "row", None),
        P("ens", None, "col", "row", None),
        P(),
        P(),
        P(),
        P(),
        P(None, "col", "row", None),
    )
    return jax.shard_map(
        local,
        mesh=mesh,
        in_specs=placed,
        out_specs=(P("ens", None, "col", "row", None), P(None, "col", "row", None)),
        check_vma=False,
    )
```

```python
import functools

import jax
import jax.numpy as jnp
from jax import lax
from jax.experimental import pallas as pl
from jax.experimental.pallas import tpu as pltpu
from jax.sharding import PartitionSpec as P

viscosity = 0.5
step_weight = 0.25
LANE = 128
in_hbm = pl.BlockSpec(memory_space=pltpu.HBM)
in_vmem = pl.BlockSpec(memory_space=pltpu.VMEM)


def hold(array):
    return pltpu.with_memory_space_constraint(array, pltpu.HBM)


def halves(value):
    high = value.astype(jnp.bfloat16)
    low = (value - high.astype(jnp.float32)).astype(jnp.bfloat16)
    return high, low


def product(left, right, contract):
    dims = ((contract[0:1], contract[1:2]), ((), ()))
    dot = functools.partial(
        lax.dot_general, dimension_numbers=dims, preferred_element_type=jnp.float32
    )
    return dot(left[0], right[0]) + (dot(left[0], right[1]) + dot(left[1], right[0]))


def pack_kernel(adj_ref, base_ref, out_ref, held_ref, slab_ref, sem_ref, out_sem_ref):
    fields, planes = adj_ref.shape[1:3]
    chunks = out_ref.shape[0] // planes
    copies = []
    for z in range(planes):
        for field in range(fields + 1):
            source = adj_ref.at[0, field, z] if field < fields else base_ref.at[0, 1, z]
            copy = pltpu.make_async_copy(source, held_ref.at[z, field], sem_ref.at[z, field])
            copy.start()
            copies.append((z, field, copy))
    sends = []
    for z, field, copy in copies:
        copy.wait()
        for chunk in range(chunks):
            slab_ref[z * chunks + chunk, field] = held_ref[z, field, :, pl.ds(chunk * LANE, LANE)]
        slabs = pl.ds(z * chunks, chunks)
        send = pltpu.make_async_copy(
            slab_ref.at[slabs, field], out_ref.at[slabs, field], out_sem_ref.at[z, field]
        )
        send.start()
        sends.append(send)
    for send in sends:
        send.wait()


def pack(adjoint, base_flow):
    _, fields, planes, rows, nx = adjoint.shape
    chunks = nx // LANE
    return pl.pallas_call(
        pack_kernel,
        in_specs=[in_hbm, in_hbm],
        out_specs=in_hbm,
        out_shape=pltpu.HBM((planes * chunks, fields + 1, rows, LANE), jnp.float32),
        scratch_shapes=[
            pltpu.VMEM((planes, fields + 1, rows, nx), jnp.float32),
            pltpu.VMEM((planes * chunks, fields + 1, rows, LANE), jnp.float32),
            pltpu.SemaphoreType.DMA((planes, fields + 1)),
            pltpu.SemaphoreType.DMA((planes, fields + 1)),
        ],
        compiler_params=pltpu.CompilerParams(vmem_limit_bytes=4 * 2**20),
        name="pack_lines",
    )(hold(adjoint), hold(base_flow))


def stream_kernel(
    adj_ref, base_ref, first_ref, second_ref, wall1_ref, wall2_ref,
    out_ref, whigh_ref, wlow_ref, high_ref, low_ref, acc_ref, sum_ref, sem_ref,
):
    step = pl.program_id(0)
    _, fields, planes, rows, nx = adj_ref.shape
    blocks = nx // LANE
    lines = fields * planes * rows

    for which, ref in enumerate((wall1_ref, wall2_ref)):
        whigh_ref[which], wlow_ref[which] = halves(ref[...])

    @pl.when(step == 0)
    def _():
        for q in range(blocks):
            block = adj_ref[0, :, :, :, pl.ds(q * LANE, LANE)].reshape(lines, LANE)
            high, low = halves(block)
            for place in (q, q + blocks):
                if place < 2 * blocks - 1:
                    high_ref[pl.ds(place * lines, lines), :] = high
                    low_ref[pl.ds(place * lines, lines), :] = low
        acc_ref[...] = jnp.zeros_like(acc_ref)

    weights = jnp.concatenate(
        [
            jnp.concatenate([first_ref[0], first_ref[1]], axis=1),
            jnp.concatenate([second_ref[0], second_ref[1]], axis=1),
        ],
        axis=0,
    )
    total = blocks * lines
    near = pl.ds(pl.multiple_of(step * (2 * lines), 2 * lines), total)
    far = pl.ds(pl.multiple_of(step * (2 * lines) + lines, lines), total)
    left = tuple(
        jnp.concatenate([ref[near, :], ref[far, :]], axis=1) for ref in (high_ref, low_ref)
    )
    acc_ref[...] += product(left, halves(weights), (1, 1))

    @pl.when(step == pl.num_programs(0) - 1)
    def _():
        for p in range(blocks):
            lanes = pl.ds(p * LANE, LANE)
            x_first = acc_ref[pl.ds(p * lines, lines), pl.ds(0, LANE)]
            x_second = acc_ref[pl.ds(p * lines, lines), pl.ds(LANE, LANE)]
            x_first = x_first.reshape(fields, planes, rows, LANE)
            x_second = x_second.reshape(fields, planes, rows, LANE)
            rhs = viscosity * x_second + base_ref[0, 0, :, :, lanes][None] * x_first
            sum_ref[:, :, :, lanes] = adj_ref[0, :, :, :, lanes] + step_weight * rhs
        copy = pltpu.make_async_copy(sum_ref, out_ref, sem_ref)
        copy.start()
        copy.wait()


def stream(adjoint, base_flow, stream_first, stream_second, wall_first, wall_second):
    _, fields, planes, rows, nx = adjoint.shape
    blocks = nx // LANE
    lines = fields * planes * rows
    steps = blocks // 2
    ny = wall_first.shape[0]
    wall_rows = ny // steps
    whole = lambda i: (0, 0, 0, 0, 0)
    return pl.pallas_call(
        stream_kernel,
        grid=(steps,),
        in_specs=[
            pl.BlockSpec((1, fields, planes, rows, nx), whole),
            pl.BlockSpec((1, 1, planes, rows, nx), whole),
            pl.BlockSpec((2, LANE, LANE), lambda i: (i, 0, 0)),
            pl.BlockSpec((2, LANE, LANE), lambda i: (i, 0, 0)),
            pl.BlockSpec((wall_rows, ny), lambda i: (i, 0)),
            pl.BlockSpec((wall_rows, ny), lambda i: (i, 0)),
        ],
        out_specs=[
            in_hbm,
            pl.BlockSpec((2, wall_rows, ny), lambda i: (0, i, 0)),
            pl.BlockSpec((2, wall_rows, ny), lambda i: (0, i, 0)),
        ],
        out_shape=[
            pltpu.HBM((fields, planes, rows, nx), jnp.float32),
            jax.ShapeDtypeStruct((2, ny, ny), jnp.bfloat16),
            jax.ShapeDtypeStruct((2, ny, ny), jnp.bfloat16),
        ],
        scratch_shapes=[
            pltpu.VMEM(((2 * blocks - 1) * lines, LANE), jnp.bfloat16),
            pltpu.VMEM(((2 * blocks - 1) * lines, LANE), jnp.bfloat16),
            pltpu.VMEM((blocks * lines, 2 * LANE), jnp.float32),
            pltpu.VMEM((fields, planes, rows, nx), jnp.float32),
            pltpu.SemaphoreType.DMA,
        ],
        compiler_params=pltpu.CompilerParams(vmem_limit_bytes=24 * 2**20),
        cost_estimate=pl.CostEstimate(
            flops=6 * 2 * lines * nx * nx, bytes_accessed=8 * 2**20, transcendentals=0
        ),
        name="stream_sweep",
    )(*map(hold, (adjoint, base_flow, stream_first, stream_second, wall_first, wall_second)))


def wall_kernel(lines_ref, whigh_ref, wlow_ref, out_ref):
    chunks, slabs, rows, _ = lines_ref.shape
    fields = slabs - 1
    ny = chunks * rows
    parts = [halves(lines_ref[:, f].reshape(ny, LANE)) for f in range(fields)]
    values = tuple(jnp.concatenate([part[k] for part in parts], axis=1) for k in range(2))
    y_first = product((whigh_ref[0], wlow_ref[0]), values, (1, 0))
    y_second = product((whigh_ref[1], wlow_ref[1]), values, (1, 0))
    speed = lines_ref[:, fields].reshape(ny, LANE)
    for f in range(fields):
        lanes = slice(f * LANE, (f + 1) * LANE)
        rhs = step_weight * (viscosity * y_second[:, lanes] + speed * y_first[:, lanes])
        out_ref[:, f] = rhs.reshape(chunks, rows, LANE)


def wall(lines, whigh, wlow):
    chunks, slabs, rows, _ = lines.shape
    ny = chunks * rows
    return pl.pallas_call(
        wall_kernel,
        in_specs=[in_vmem, in_vmem, in_vmem],
        out_specs=in_vmem,
        out_shape=jax.ShapeDtypeStruct((chunks, slabs - 1, rows, LANE), jnp.float32),
        compiler_params=pltpu.CompilerParams(vmem_limit_bytes=8 * 2**20),
        cost_estimate=pl.CostEstimate(
            flops=6 * 2 * ny * ny * LANE * (slabs - 1), bytes_accessed=4 * 2**20, transcendentals=0
        ),
        name="wall_sweep",
    )(lines, whigh, wlow)


def update_kernel(stream_ref, wall_ref, other_ref, forcing_ref, out_ref, early_ref):
    for chunk in range(wall_ref.shape[0]):
        lanes = pl.ds(chunk * LANE, LANE)
        updated = stream_ref[:, 0, :, lanes] + wall_ref[chunk]
        out_ref[0, :, 0, :, lanes] = updated
        early_ref[:, 0, :, lanes] = forcing_ref[:, 0, :, lanes] * (
            updated + other_ref[:, 0, :, lanes]
        )


def update(streamed, walled, other_streamed, forcing):
    fields, planes, rows, nx = streamed.shape
    chunks = nx // LANE
    held = pl.BlockSpec((fields, 1, rows, nx), lambda z: (0, z, 0, 0))
    return pl.pallas_call(
        update_kernel,
        grid=(planes,),
        in_specs=[held, pl.BlockSpec((chunks, fields, rows, LANE), lambda z: (z, 0, 0, 0)), held, held],
        out_specs=[pl.BlockSpec((1, fields, 1, rows, nx), lambda z: (0, 0, z, 0, 0)), held],
        out_shape=[
            jax.ShapeDtypeStruct((1, fields, planes, rows, nx), jnp.float32),
            jax.ShapeDtypeStruct((fields, planes, rows, nx), jnp.float32),
        ],
        compiler_params=pltpu.CompilerParams(vmem_limit_bytes=8 * 2**20),
        name="add_sweeps",
    )(streamed, walled, other_streamed, forcing)


def gradient_kernel(early_ref, forcing_ref, wall_ref, out_ref, held_ref, sem_ref):
    fields, planes, rows, nx = early_ref.shape
    chunks = nx // LANE
    copies = []
    for z in range(planes):
        for field in range(fields):
            for chunk in range(chunks):
                lanes = pl.ds(chunk * LANE, LANE)
                held_ref[field, z, :, lanes] = (
                    early_ref[field, z, :, lanes]
                    + forcing_ref[field, z, :, lanes] * wall_ref[z * chunks + chunk, field]
                )
            copy = pltpu.make_async_copy(
                held_ref.at[field, z], out_ref.at[field, z], sem_ref.at[field, z]
            )
            copy.start()
            copies.append(copy)
    for copy in copies:
        copy.wait()


def gradient(early, forcing, other_walled):
    return pl.pallas_call(
        gradient_kernel,
        in_specs=[in_vmem, in_vmem, in_vmem],
        out_specs=in_hbm,
        out_shape=jax.ShapeDtypeStruct(early.shape, jnp.float32),
        scratch_shapes=[
            pltpu.VMEM(early.shape, jnp.float32),
            pltpu.SemaphoreType.DMA(early.shape[:2]),
        ],
        compiler_params=pltpu.CompilerParams(vmem_limit_bytes=4 * 2**20),
        name="body_force",
    )(early, forcing, other_walled)


def local(adjoint, base_flow, stream_first, stream_second, wall_first, wall_second, forcing):
    swap = [(0, 1), (1, 0)]
    lines = lax.all_to_all(pack(adjoint, base_flow), "row", 0, 0)
    streamed, whigh, wlow = stream(
        adjoint, base_flow, stream_first, stream_second, wall_first, wall_second
    )
    other_streamed = lax.ppermute(streamed, "ens", swap)
    walled = lax.all_to_all(wall(lines, whigh, wlow), "row", 0, 0)
    other_walled = lax.ppermute(walled, "ens", swap)
    updated, early = update(streamed, walled, other_streamed, forcing)
    return updated, gradient(early, forcing, other_walled)


def solution(mesh):
    placed = (
        P("ens", None, "col", "row", None),
        P("ens", None, "col", "row", None),
        P(),
        P(),
        P(),
        P(),
        P(None, "col", "row", None),
    )
    return jax.shard_map(
        local,
        mesh=mesh,
        in_specs=placed,
        out_specs=(P("ens", None, "col", "row", None), P(None, "col", "row", None)),
        check_vma=False,
    )
```

```python
import functools

import jax
import jax.numpy as jnp
from jax import lax
from jax.experimental import pallas as pl
from jax.experimental.pallas import tpu as pltpu
from jax.sharding import PartitionSpec as P

viscosity = 0.5
step_weight = 0.25
LANE = 128
PIECES = 2
in_hbm = pl.BlockSpec(memory_space=pltpu.HBM)
in_vmem = pl.BlockSpec(memory_space=pltpu.VMEM)


def hold(array):
    return pltpu.with_memory_space_constraint(array, pltpu.HBM)


def halves(value):
    high = value.astype(jnp.bfloat16)
    low = (value - high.astype(jnp.float32)).astype(jnp.bfloat16)
    return high, low


def product(left, right, contract):
    dims = ((contract[0:1], contract[1:2]), ((), ()))
    dot = functools.partial(
        lax.dot_general, dimension_numbers=dims, preferred_element_type=jnp.float32
    )
    return dot(left[0], right[0]) + (dot(left[0], right[1]) + dot(left[1], right[0]))


def pack_kernel(adj_ref, base_ref, after_ref, out_ref, held_ref, slab_ref, sem_ref, out_sem_ref):
    fields, planes = adj_ref.shape[1:3]
    chunks = out_ref.shape[0] // planes
    parts = out_sem_ref.shape[1]
    count = chunks // parts
    copies = []
    for z in range(planes):
        for field in range(fields + 1):
            source = adj_ref.at[0, field, z] if field < fields else base_ref.at[0, 1, z]
            copy = pltpu.make_async_copy(source, held_ref.at[z, field], sem_ref.at[z, field])
            copy.start()
            copies.append(copy)
    sends = []
    for z in range(planes):
        for copy in copies[z * (fields + 1) : (z + 1) * (fields + 1)]:
            copy.wait()
        for part in range(parts):
            for chunk in range(part * count, (part + 1) * count):
                slab_ref[z * chunks + chunk] = held_ref[z, :, :, pl.ds(chunk * LANE, LANE)]
            slabs = pl.ds(z * chunks + part * count, count)
            send = pltpu.make_async_copy(
                slab_ref.at[slabs], out_ref.at[slabs], out_sem_ref.at[z, part]
            )
            send.start()
            sends.append(send)
    for send in sends:
        send.wait()


def pack(adjoint, base_flow, after):
    _, fields, planes, rows, nx = adjoint.shape
    chunks = nx // LANE
    return pl.pallas_call(
        pack_kernel,
        in_specs=[in_hbm, in_hbm, in_hbm],
        out_specs=in_hbm,
        out_shape=pltpu.HBM((planes * chunks, fields + 1, rows, LANE), jnp.float32),
        scratch_shapes=[
            pltpu.VMEM((planes, fields + 1, rows, nx), jnp.float32),
            pltpu.VMEM((planes * chunks, fields + 1, rows, LANE), jnp.float32),
            pltpu.SemaphoreType.DMA((planes, fields + 1)),
            pltpu.SemaphoreType.DMA((planes, 4)),
        ],
        compiler_params=pltpu.CompilerParams(vmem_limit_bytes=4 * 2**20),
        name="pack_lines",
    )(hold(adjoint), hold(base_flow), hold(after))


def stream_kernel(turn, *refs):
    adj_ref, base_ref, first_ref, second_ref = refs[:4]
    extra = 4 * turn
    scratch = refs[len(refs) - 8 - extra :]
    field_ref, speed_ref, first, second, high_ref, low_ref, acc_ref, sem_ref = scratch[:8]
    outs = refs[len(refs) - 9 - extra - 2 * turn : len(refs) - 8 - extra]
    out_ref = outs[0]
    fields, planes, rows, nx = field_ref.shape
    blocks = nx // LANE
    lines = fields * planes * rows

    mine = lax.rem(lax.axis_index("col"), 2) == turn

    @pl.when(mine)
    def _():
        loads = [
            pltpu.make_async_copy(source, target, sem_ref.at[k])
            for k, (source, target) in enumerate(
                (
                    (adj_ref.at[0], field_ref),
                    (base_ref.at[0, 0], speed_ref),
                    (first_ref, first),
                    (second_ref, second),
                )
            )
        ]
        for load in loads:
            load.start()
        loads[0].wait()
        for q in range(blocks):
            block = field_ref[:, :, :, pl.ds(q * LANE, LANE)].reshape(lines, LANE)
            high, low = halves(block)
            for place in (q, q + blocks):
                if place < 2 * blocks - 1:
                    high_ref[pl.ds(place * lines, lines), :] = high
                    low_ref[pl.ds(place * lines, lines), :] = low
        acc_ref[...] = jnp.zeros_like(acc_ref)
        for load in loads[1:]:
            load.wait()

        @pl.loop(0, blocks // 2)
        def _(step):
            weights = jnp.concatenate(
                [
                    jnp.concatenate([ref[2 * step], ref[2 * step + 1]], axis=1)
                    for ref in (first, second)
                ],
                axis=0,
            )
            total = blocks * lines
            near = pl.ds(pl.multiple_of(step * (2 * lines), 2 * lines), total)
            far = pl.ds(pl.multiple_of(step * (2 * lines) + lines, lines), total)
            left = tuple(
                jnp.concatenate([ref[near, :], ref[far, :]], axis=1) for ref in (high_ref, low_ref)
            )
            acc_ref[...] += product(left, halves(weights), (1, 1))

        for p in range(blocks):
            lanes = pl.ds(p * LANE, LANE)
            x_first = acc_ref[pl.ds(p * lines, lines), pl.ds(0, LANE)]
            x_second = acc_ref[pl.ds(p * lines, lines), pl.ds(LANE, LANE)]
            x_first = x_first.reshape(fields, planes, rows, LANE)
            x_second = x_second.reshape(fields, planes, rows, LANE)
            rhs = viscosity * x_second + speed_ref[:, :, lanes][None] * x_first
            target = out_ref if turn == 0 else field_ref
            target[:, :, :, lanes] = field_ref[:, :, :, lanes] + step_weight * rhs
        if turn == 0:
            return
        copy = pltpu.make_async_copy(field_ref, out_ref, sem_ref.at[0])
        copy.start()
        copy.wait()
        if turn == 1:
            split_operators(refs[4:6], outs[1:], *scratch[8:])

    if turn == 0:

        @pl.when(jnp.logical_not(mine))
        def _():
            copy = pltpu.make_async_copy(refs[4], out_ref, sem_ref.at[0])
            copy.start()
            copy.wait()


def split_operators(wall_refs, out_refs, value_ref, whigh_ref, wlow_ref, sem_ref):
    loads = [
        pltpu.make_async_copy(ref, value_ref.at[k], sem_ref.at[k])
        for k, ref in enumerate(wall_refs)
    ]
    for load in loads:
        load.start()
    for which, load in enumerate(loads):
        load.wait()
        whigh_ref[which], wlow_ref[which] = halves(value_ref[which])
    stores = [
        pltpu.make_async_copy(ref, out, sem_ref.at[k])
        for k, (ref, out) in enumerate(zip((whigh_ref, wlow_ref), out_refs))
    ]
    for store in stores:
        store.start()
    for store in stores:
        store.wait()


def stream(turn, adjoint, base_flow, stream_first, stream_second, walls=(), before=None):
    _, fields, planes, rows, nx = adjoint.shape
    blocks = nx // LANE
    lines = fields * planes * rows
    operands = [adjoint, base_flow, stream_first, stream_second, *walls]
    shapes = [jax.ShapeDtypeStruct((fields, planes, rows, nx), jnp.float32)]
    scratch = []
    if turn == 1:
        both = (2, *walls[0].shape)
        shapes = [pltpu.HBM((fields, planes, rows, nx), jnp.float32)]
        shapes += [pltpu.HBM(both, jnp.bfloat16)] * 2
        scratch = [
            pltpu.VMEM(both, jnp.float32),
            pltpu.VMEM(both, jnp.bfloat16),
            pltpu.VMEM(both, jnp.bfloat16),
            pltpu.SemaphoreType.DMA((2,)),
        ]
    if before is not None:
        operands.append(before)
    return pl.pallas_call(
        functools.partial(stream_kernel, turn),
        in_specs=[in_hbm] * len(operands),
        out_specs=[in_hbm if turn == 1 else in_vmem] * len(shapes),
        out_shape=shapes,
        scratch_shapes=[
            pltpu.VMEM((fields, planes, rows, nx), jnp.float32),
            pltpu.VMEM((planes, rows, nx), jnp.float32),
            pltpu.VMEM(stream_first.shape, jnp.float32),
            pltpu.VMEM(stream_second.shape, jnp.float32),
            pltpu.VMEM(((2 * blocks - 1) * lines, LANE), jnp.bfloat16),
            pltpu.VMEM(((2 * blocks - 1) * lines, LANE), jnp.bfloat16),
            pltpu.VMEM((blocks * lines, 2 * LANE), jnp.float32),
            pltpu.SemaphoreType.DMA((4,)),
        ]
        + scratch,
        compiler_params=pltpu.CompilerParams(vmem_limit_bytes=28 * 2**20),
        cost_estimate=pl.CostEstimate(
            flops=6 * 2 * lines * nx * nx, bytes_accessed=8 * 2**20, transcendentals=0
        ),
        name="stream_sweep",
    )(*map(hold, operands))


def split_kernel(wall1_ref, wall2_ref, had1_ref, had2_ref, whigh_ref, wlow_ref, value_ref, sem_ref):
    late = lax.rem(lax.axis_index("col"), 2) == 1

    @pl.when(late)
    def _():
        loads = [
            pltpu.make_async_copy(source, target, sem_ref.at[k])
            for k, (source, target) in enumerate(((had1_ref, whigh_ref), (had2_ref, wlow_ref)))
        ]
        for load in loads:
            load.start()
        for load in loads:
            load.wait()

    @pl.when(jnp.logical_not(late))
    def _():
        loads = [
            pltpu.make_async_copy(ref, value_ref.at[k], sem_ref.at[k])
            for k, ref in enumerate((wall1_ref, wall2_ref))
        ]
        for load in loads:
            load.start()
        for which, load in enumerate(loads):
            load.wait()
            whigh_ref[which], wlow_ref[which] = halves(value_ref[which])


def split(wall_first, wall_second, whigh, wlow):
    return pl.pallas_call(
        split_kernel,
        in_specs=[in_hbm] * 4,
        out_specs=[in_vmem] * 2,
        out_shape=[jax.ShapeDtypeStruct(whigh.shape, jnp.bfloat16)] * 2,
        scratch_shapes=[pltpu.VMEM(whigh.shape, jnp.float32), pltpu.SemaphoreType.DMA((2,))],
        compiler_params=pltpu.CompilerParams(vmem_limit_bytes=8 * 2**20),
        cost_estimate=pl.CostEstimate(flops=2**21, bytes_accessed=4 * 2**20, transcendentals=0),
        name="split_wall",
    )(*map(hold, (wall_first, wall_second, whigh, wlow)))


def wall_kernel(lines_ref, whigh_ref, wlow_ref, out_ref, held_ref, sem_ref):
    chunks, slabs, rows, _ = lines_ref.shape
    fields = slabs - 1
    ny = chunks * rows
    parts = [halves(lines_ref[:, f].reshape(ny, LANE)) for f in range(fields)]
    values = jnp.concatenate([part[k] for k in range(2) for part in parts], axis=1)
    width = fields * LANE
    dot = functools.partial(jnp.dot, preferred_element_type=jnp.float32)
    pieces = sem_ref.shape[0]
    length, count = ny // pieces, chunks // pieces
    copies = []
    for piece in range(pieces):
        own, slab = pl.ds(piece * length, length), pl.ds(piece * count, count)
        weights = tuple(
            jnp.concatenate([ref[0, own, :], ref[1, own, :]], axis=0)
            for ref in (whigh_ref, wlow_ref)
        )
        both = dot(weights[0], values)
        both = both[:, :width] + (both[:, width:] + dot(weights[1], values[:, :width]))
        speed = lines_ref[slab, fields].reshape(length, LANE)
        for f in range(fields):
            lanes = slice(f * LANE, (f + 1) * LANE)
            rhs = step_weight * (
                viscosity * both[length:, lanes] + speed * both[:length, lanes]
            )
            held_ref[slab, f] = rhs.reshape(count, rows, LANE)
        copy = pltpu.make_async_copy(held_ref.at[slab], out_ref.at[slab], sem_ref.at[piece])
        copy.start()
        copies.append(copy)
    for copy in copies:
        copy.wait()


def wall(lines, whigh, wlow):
    chunks, slabs, rows, _ = lines.shape
    ny = chunks * rows
    shape = (chunks, slabs - 1, rows, LANE)
    return pl.pallas_call(
        wall_kernel,
        in_specs=[in_vmem, in_vmem, in_vmem],
        out_specs=in_hbm,
        out_shape=pltpu.HBM(shape, jnp.float32),
        scratch_shapes=[
            pltpu.VMEM(shape, jnp.float32),
            pltpu.SemaphoreType.DMA((PIECES,)),
        ],
        compiler_params=pltpu.CompilerParams(vmem_limit_bytes=12 * 2**20),
        cost_estimate=pl.CostEstimate(
            flops=6 * 2 * ny * ny * LANE * (slabs - 1), bytes_accessed=4 * 2**20, transcendentals=0
        ),
        name="wall_sweep",
    )(lines, whigh, wlow)


def update_kernel(stream_ref, wall_ref, out_ref, held_ref, sem_ref):
    fields, planes, rows, nx = held_ref.shape
    chunks = nx // LANE
    stores = []
    for z in range(planes):
        for field in range(fields):
            for chunk in range(chunks):
                lanes = pl.ds(chunk * LANE, LANE)
                held_ref[field, z, :, lanes] = (
                    stream_ref[field, z, :, lanes] + wall_ref[z * chunks + chunk, field]
                )
            store = pltpu.make_async_copy(
                held_ref.at[field, z], out_ref.at[0, field, z], sem_ref.at[field, z]
            )
            store.start()
            stores.append(store)
    for store in stores:
        store.wait()


def update(streamed, walled):
    return pl.pallas_call(
        update_kernel,
        in_specs=[in_vmem, in_vmem],
        out_specs=in_hbm,
        out_shape=pltpu.HBM((1, *streamed.shape), jnp.float32),
        scratch_shapes=[
            pltpu.VMEM(streamed.shape, jnp.float32),
            pltpu.SemaphoreType.DMA(streamed.shape[:2]),
        ],
        compiler_params=pltpu.CompilerParams(vmem_limit_bytes=4 * 2**20),
        name="add_sweeps",
    )(streamed, walled)


def gradient_kernel(early_ref, forcing_ref, other_ref, out_ref, held_ref, sem_ref):
    fields, planes = forcing_ref.shape[:2]
    copies = []
    for field in range(fields):
        for z in range(planes):
            held_ref[field, z] = (
                early_ref[field, z] + forcing_ref[field, z] * other_ref[0, field, z]
            )
            copy = pltpu.make_async_copy(
                held_ref.at[field, z], out_ref.at[field, z], sem_ref.at[field, z]
            )
            copy.start()
            copies.append(copy)
    for copy in copies:
        copy.wait()


def gradient(early, forcing, other):
    return pl.pallas_call(
        gradient_kernel,
        in_specs=[in_vmem, in_vmem, in_vmem],
        out_specs=in_hbm,
        out_shape=jax.ShapeDtypeStruct(forcing.shape, jnp.float32),
        scratch_shapes=[
            pltpu.VMEM(forcing.shape, jnp.float32),
            pltpu.SemaphoreType.DMA(forcing.shape[:2]),
        ],
        compiler_params=pltpu.CompilerParams(vmem_limit_bytes=4 * 2**20),
        name="body_force",
    )(early, forcing, other)


def local(adjoint, base_flow, stream_first, stream_second, wall_first, wall_second, forcing):
    operators = (stream_first, stream_second)
    walls = (wall_first, wall_second)
    streamed, whigh, wlow = stream(1, adjoint, base_flow, *operators, walls=walls)
    lines = lax.all_to_all(pack(adjoint, base_flow, streamed), "row", 0, 0)
    (streamed,) = stream(0, adjoint, base_flow, *operators, before=streamed)
    whigh, wlow = split(*walls, whigh, wlow)
    walled = lax.all_to_all(wall(lines, whigh, wlow), "row", 0, 0)
    updated = update(streamed, walled)
    other = lax.ppermute(updated, "ens", [(0, 1), (1, 0)])
    return updated, gradient(forcing * updated[0], forcing, other)


def solution(mesh):
    placed = (
        P("ens", None, "col", "row", None),
        P("ens", None, "col", "row", None),
        P(),
        P(),
        P(),
        P(),
        P(None, "col", "row", None),
    )
    return jax.shard_map(
        local,
        mesh=mesh,
        in_specs=placed,
        out_specs=(P("ens", None, "col", "row", None), P(None, "col", "row", None)),
        check_vma=False,
    )
```

```python
import functools

import jax
import jax.numpy as jnp
from jax import lax
from jax.experimental import pallas as pl
from jax.experimental.pallas import tpu as pltpu
from jax.sharding import PartitionSpec as P

viscosity = 0.5
step_weight = 0.25
LANE = 128
PIECES = 2
in_hbm = pl.BlockSpec(memory_space=pltpu.HBM)
in_vmem = pl.BlockSpec(memory_space=pltpu.VMEM)


def hold(array):
    return pltpu.with_memory_space_constraint(array, pltpu.HBM)


def halves(value):
    high = value.astype(jnp.bfloat16)
    low = (value - high.astype(jnp.float32)).astype(jnp.bfloat16)
    return high, low


def product(left, right, contract):
    dims = ((contract[0:1], contract[1:2]), ((), ()))
    dot = functools.partial(
        lax.dot_general, dimension_numbers=dims, preferred_element_type=jnp.float32
    )
    return dot(left[0], right[0]) + (dot(left[0], right[1]) + dot(left[1], right[0]))


def pack_kernel(adj_ref, base_ref, after_ref, out_ref, held_ref, slab_ref, sem_ref, out_sem_ref):
    fields, planes = adj_ref.shape[1:3]
    chunks = out_ref.shape[0] // planes
    parts = out_sem_ref.shape[1]
    count = chunks // parts
    copies = []
    for z in range(planes):
        for field in range(fields + 1):
            source = adj_ref.at[0, field, z] if field < fields else base_ref.at[0, 1, z]
            copy = pltpu.make_async_copy(source, held_ref.at[z, field], sem_ref.at[z, field])
            copy.start()
            copies.append(copy)
    sends = []
    for z in range(planes):
        for copy in copies[z * (fields + 1) : (z + 1) * (fields + 1)]:
            copy.wait()
        for part in range(parts):
            for chunk in range(part * count, (part + 1) * count):
                slab_ref[z * chunks + chunk] = held_ref[z, :, :, pl.ds(chunk * LANE, LANE)]
            slabs = pl.ds(z * chunks + part * count, count)
            send = pltpu.make_async_copy(
                slab_ref.at[slabs], out_ref.at[slabs], out_sem_ref.at[z, part]
            )
            send.start()
            sends.append(send)
    for send in sends:
        send.wait()


def pack(adjoint, base_flow, after):
    _, fields, planes, rows, nx = adjoint.shape
    chunks = nx // LANE
    return pl.pallas_call(
        pack_kernel,
        in_specs=[in_hbm, in_hbm, in_hbm],
        out_specs=in_hbm,
        out_shape=pltpu.HBM((planes * chunks, fields + 1, rows, LANE), jnp.float32),
        scratch_shapes=[
            pltpu.VMEM((planes, fields + 1, rows, nx), jnp.float32),
            pltpu.VMEM((planes * chunks, fields + 1, rows, LANE), jnp.float32),
            pltpu.SemaphoreType.DMA((planes, fields + 1)),
            pltpu.SemaphoreType.DMA((planes, 4)),
        ],
        compiler_params=pltpu.CompilerParams(vmem_limit_bytes=4 * 2**20),
        name="pack_lines",
    )(hold(adjoint), hold(base_flow), hold(after))


def stream_kernel(turn, *refs):
    adj_ref, base_ref, first_ref, second_ref = refs[:4]
    extra = 4 * turn
    scratch = refs[len(refs) - 8 - extra :]
    field_ref, speed_ref, first, second, high_ref, low_ref, acc_ref, sem_ref = scratch[:8]
    outs = refs[len(refs) - 9 - extra - 2 * turn : len(refs) - 8 - extra]
    out_ref = outs[0]
    fields, planes, rows, nx = field_ref.shape
    blocks = nx // LANE
    lines = fields * planes * rows

    mine = lax.rem(lax.axis_index("col"), 2) == turn

    @pl.when(mine)
    def _():
        loads = [
            pltpu.make_async_copy(source, target, sem_ref.at[k])
            for k, (source, target) in enumerate(
                (
                    (adj_ref.at[0], field_ref),
                    (base_ref.at[0, 0], speed_ref),
                    (first_ref, first),
                    (second_ref, second),
                )
            )
        ]
        for load in loads:
            load.start()
        loads[0].wait()
        for q in range(blocks):
            block = field_ref[:, :, :, pl.ds(q * LANE, LANE)].reshape(lines, LANE)
            high, low = halves(block)
            for place in (q, q + blocks):
                if place < 2 * blocks - 1:
                    high_ref[pl.ds(place * lines, lines), :] = high
                    low_ref[pl.ds(place * lines, lines), :] = low
        acc_ref[...] = jnp.zeros_like(acc_ref)
        for load in loads[1:]:
            load.wait()

        @pl.loop(0, blocks // 2)
        def _(step):
            weights = jnp.concatenate(
                [
                    jnp.concatenate([ref[2 * step], ref[2 * step + 1]], axis=1)
                    for ref in (first, second)
                ],
                axis=0,
            )
            total = blocks * lines
            near = pl.ds(pl.multiple_of(step * (2 * lines), 2 * lines), total)
            far = pl.ds(pl.multiple_of(step * (2 * lines) + lines, lines), total)
            left = tuple(
                jnp.concatenate([ref[near, :], ref[far, :]], axis=1) for ref in (high_ref, low_ref)
            )
            acc_ref[...] += product(left, halves(weights), (1, 1))

        for p in range(blocks):
            lanes = pl.ds(p * LANE, LANE)
            x_first = acc_ref[pl.ds(p * lines, lines), pl.ds(0, LANE)]
            x_second = acc_ref[pl.ds(p * lines, lines), pl.ds(LANE, LANE)]
            x_first = x_first.reshape(fields, planes, rows, LANE)
            x_second = x_second.reshape(fields, planes, rows, LANE)
            rhs = viscosity * x_second + speed_ref[:, :, lanes][None] * x_first
            target = out_ref if turn == 0 else field_ref
            target[:, :, :, lanes] = field_ref[:, :, :, lanes] + step_weight * rhs
        if turn == 0:
            return
        copy = pltpu.make_async_copy(field_ref, out_ref, sem_ref.at[0])
        copy.start()
        copy.wait()
        if turn == 1:
            split_operators(refs[4:6], outs[1:], *scratch[8:])

    if turn == 0:

        @pl.when(jnp.logical_not(mine))
        def _():
            copy = pltpu.make_async_copy(refs[4], out_ref, sem_ref.at[0])
            copy.start()
            copy.wait()


def split_operators(wall_refs, out_refs, value_ref, whigh_ref, wlow_ref, sem_ref):
    loads = [
        pltpu.make_async_copy(ref, value_ref.at[k], sem_ref.at[k])
        for k, ref in enumerate(wall_refs)
    ]
    for load in loads:
        load.start()
    for which, load in enumerate(loads):
        load.wait()
        whigh_ref[which], wlow_ref[which] = halves(value_ref[which])
    stores = [
        pltpu.make_async_copy(ref, out, sem_ref.at[k])
        for k, (ref, out) in enumerate(zip((whigh_ref, wlow_ref), out_refs))
    ]
    for store in stores:
        store.start()
    for store in stores:
        store.wait()


def stream(turn, adjoint, base_flow, stream_first, stream_second, walls=(), before=None):
    _, fields, planes, rows, nx = adjoint.shape
    blocks = nx // LANE
    lines = fields * planes * rows
    operands = [adjoint, base_flow, stream_first, stream_second, *walls]
    shapes = [jax.ShapeDtypeStruct((fields, planes, rows, nx), jnp.float32)]
    scratch = []
    if turn == 1:
        both = (2, *walls[0].shape)
        shapes = [pltpu.HBM((fields, planes, rows, nx), jnp.float32)]
        shapes += [pltpu.HBM(both, jnp.bfloat16)] * 2
        scratch = [
            pltpu.VMEM(both, jnp.float32),
            pltpu.VMEM(both, jnp.bfloat16),
            pltpu.VMEM(both, jnp.bfloat16),
            pltpu.SemaphoreType.DMA((2,)),
        ]
    if before is not None:
        operands.append(before)
    return pl.pallas_call(
        functools.partial(stream_kernel, turn),
        in_specs=[in_hbm] * len(operands),
        out_specs=[in_hbm if turn == 1 else in_vmem] * len(shapes),
        out_shape=shapes,
        scratch_shapes=[
            pltpu.VMEM((fields, planes, rows, nx), jnp.float32),
            pltpu.VMEM((planes, rows, nx), jnp.float32),
            pltpu.VMEM(stream_first.shape, jnp.float32),
            pltpu.VMEM(stream_second.shape, jnp.float32),
            pltpu.VMEM(((2 * blocks - 1) * lines, LANE), jnp.bfloat16),
            pltpu.VMEM(((2 * blocks - 1) * lines, LANE), jnp.bfloat16),
            pltpu.VMEM((blocks * lines, 2 * LANE), jnp.float32),
            pltpu.SemaphoreType.DMA((4,)),
        ]
        + scratch,
        compiler_params=pltpu.CompilerParams(vmem_limit_bytes=28 * 2**20),
        cost_estimate=pl.CostEstimate(
            flops=6 * 2 * lines * nx * nx, bytes_accessed=8 * 2**20, transcendentals=0
        ),
        name="stream_sweep",
    )(*map(hold, operands))


def split_kernel(wall1_ref, wall2_ref, had1_ref, had2_ref, whigh_ref, wlow_ref, value_ref, sem_ref):
    late = lax.rem(lax.axis_index("col"), 2) == 1

    @pl.when(late)
    def _():
        loads = [
            pltpu.make_async_copy(source, target, sem_ref.at[k])
            for k, (source, target) in enumerate(((had1_ref, whigh_ref), (had2_ref, wlow_ref)))
        ]
        for load in loads:
            load.start()
        for load in loads:
            load.wait()

    @pl.when(jnp.logical_not(late))
    def _():
        loads = [
            pltpu.make_async_copy(ref, value_ref.at[k], sem_ref.at[k])
            for k, ref in enumerate((wall1_ref, wall2_ref))
        ]
        for load in loads:
            load.start()
        for which, load in enumerate(loads):
            load.wait()
            whigh_ref[which], wlow_ref[which] = halves(value_ref[which])


def split(wall_first, wall_second, whigh, wlow):
    return pl.pallas_call(
        split_kernel,
        in_specs=[in_hbm] * 4,
        out_specs=[in_vmem] * 2,
        out_shape=[jax.ShapeDtypeStruct(whigh.shape, jnp.bfloat16)] * 2,
        scratch_shapes=[pltpu.VMEM(whigh.shape, jnp.float32), pltpu.SemaphoreType.DMA((2,))],
        compiler_params=pltpu.CompilerParams(vmem_limit_bytes=8 * 2**20),
        cost_estimate=pl.CostEstimate(flops=2**21, bytes_accessed=4 * 2**20, transcendentals=0),
        name="split_wall",
    )(*map(hold, (wall_first, wall_second, whigh, wlow)))


def wall_kernel(lines_ref, whigh_ref, wlow_ref, out_ref, held_ref, sem_ref):
    chunks, slabs, rows, _ = lines_ref.shape
    fields = slabs - 1
    ny = chunks * rows
    parts = [halves(lines_ref[:, f].reshape(ny, LANE)) for f in range(fields)]
    values = jnp.concatenate([part[k] for k in range(2) for part in parts], axis=1)
    width = fields * LANE
    dot = functools.partial(jnp.dot, preferred_element_type=jnp.float32)
    pieces = sem_ref.shape[0]
    length, count = ny // pieces, chunks // pieces
    copies = []
    for piece in range(pieces):
        own, slab = pl.ds(piece * length, length), pl.ds(piece * count, count)
        weights = tuple(
            jnp.concatenate([ref[0, own, :], ref[1, own, :]], axis=0)
            for ref in (whigh_ref, wlow_ref)
        )
        both = dot(weights[0], values)
        both = both[:, :width] + (both[:, width:] + dot(weights[1], values[:, :width]))
        speed = lines_ref[slab, fields].reshape(length, LANE)
        for f in range(fields):
            lanes = slice(f * LANE, (f + 1) * LANE)
            rhs = step_weight * (
                viscosity * both[length:, lanes] + speed * both[:length, lanes]
            )
            held_ref[slab, f] = rhs.reshape(count, rows, LANE)
        copy = pltpu.make_async_copy(held_ref.at[slab], out_ref.at[slab], sem_ref.at[piece])
        copy.start()
        copies.append(copy)
    for copy in copies:
        copy.wait()


def wall(lines, whigh, wlow):
    chunks, slabs, rows, _ = lines.shape
    ny = chunks * rows
    shape = (chunks, slabs - 1, rows, LANE)
    return pl.pallas_call(
        wall_kernel,
        in_specs=[in_vmem, in_vmem, in_vmem],
        out_specs=in_hbm,
        out_shape=pltpu.HBM(shape, jnp.float32),
        scratch_shapes=[
            pltpu.VMEM(shape, jnp.float32),
            pltpu.SemaphoreType.DMA((PIECES,)),
        ],
        compiler_params=pltpu.CompilerParams(vmem_limit_bytes=12 * 2**20),
        cost_estimate=pl.CostEstimate(
            flops=6 * 2 * ny * ny * LANE * (slabs - 1), bytes_accessed=4 * 2**20, transcendentals=0
        ),
        name="wall_sweep",
    )(lines, whigh, wlow)


def update_kernel(stream_ref, wall_ref, out_ref):
    fields, planes, rows, nx = out_ref.shape
    chunks = nx // LANE
    for chunk in range(chunks):
        lanes = pl.ds(chunk * LANE, LANE)
        for z in range(planes):
            for field in range(fields):
                out_ref[field, z, :, lanes] = (
                    stream_ref[field, z, :, lanes] + wall_ref[z * chunks + chunk, field]
                )


def update(streamed, walled):
    return pl.pallas_call(
        update_kernel,
        in_specs=[in_vmem, in_vmem],
        out_specs=in_vmem,
        out_shape=jax.ShapeDtypeStruct(streamed.shape, jnp.float32),
        compiler_params=pltpu.CompilerParams(vmem_limit_bytes=4 * 2**20),
        name="add_sweeps",
    )(streamed, walled)


def keep_kernel(updated_ref, forcing_ref, out_ref, early_ref, sem_ref):
    copy = pltpu.make_async_copy(updated_ref, out_ref.at[0], sem_ref)
    copy.start()
    early_ref[...] = forcing_ref[...] * updated_ref[...]
    copy.wait()


def keep(updated, forcing):
    return pl.pallas_call(
        keep_kernel,
        in_specs=[in_vmem, in_vmem],
        out_specs=[in_hbm, in_vmem],
        out_shape=[
            pltpu.HBM((1, *updated.shape), jnp.float32),
            jax.ShapeDtypeStruct(updated.shape, jnp.float32),
        ],
        scratch_shapes=[pltpu.SemaphoreType.DMA],
        compiler_params=pltpu.CompilerParams(vmem_limit_bytes=4 * 2**20),
        name="keep_updated",
    )(updated, forcing)


def gradient_kernel(early_ref, forcing_ref, other_ref, out_ref, held_ref, sem_ref):
    fields, planes = forcing_ref.shape[:2]
    copies = []
    for field in range(fields):
        for z in range(planes):
            held_ref[field, z] = (
                early_ref[field, z] + forcing_ref[field, z] * other_ref[field, z]
            )
            copy = pltpu.make_async_copy(
                held_ref.at[field, z], out_ref.at[field, z], sem_ref.at[field, z]
            )
            copy.start()
            copies.append(copy)
    for copy in copies:
        copy.wait()


def gradient(early, forcing, other):
    return pl.pallas_call(
        gradient_kernel,
        in_specs=[in_vmem, in_vmem, in_vmem],
        out_specs=in_hbm,
        out_shape=jax.ShapeDtypeStruct(forcing.shape, jnp.float32),
        scratch_shapes=[
            pltpu.VMEM(forcing.shape, jnp.float32),
            pltpu.SemaphoreType.DMA(forcing.shape[:2]),
        ],
        compiler_params=pltpu.CompilerParams(vmem_limit_bytes=4 * 2**20),
        name="body_force",
    )(early, forcing, other)


def local(adjoint, base_flow, stream_first, stream_second, wall_first, wall_second, forcing):
    operators = (stream_first, stream_second)
    walls = (wall_first, wall_second)
    streamed, whigh, wlow = stream(1, adjoint, base_flow, *operators, walls=walls)
    lines = lax.all_to_all(pack(adjoint, base_flow, streamed), "row", 0, 0)
    (streamed,) = stream(0, adjoint, base_flow, *operators, before=streamed)
    whigh, wlow = split(*walls, whigh, wlow)
    walled = lax.all_to_all(wall(lines, whigh, wlow), "row", 0, 0)
    updated = update(streamed, walled)
    other = lax.ppermute(updated, "ens", [(0, 1), (1, 0)])
    kept, early = keep(updated, forcing)
    return kept, gradient(early, forcing, other)


def solution(mesh):
    placed = (
        P("ens", None, "col", "row", None),
        P("ens", None, "col", "row", None),
        P(),
        P(),
        P(),
        P(),
        P(None, "col", "row", None),
    )
    return jax.shard_map(
        local,
        mesh=mesh,
        in_specs=placed,
        out_specs=(P("ens", None, "col", "row", None), P(None, "col", "row", None)),
        check_vma=False,
    )
```

```python
import functools

import jax
import jax.numpy as jnp
from jax import lax
from jax.experimental import pallas as pl
from jax.experimental.pallas import tpu as pltpu
from jax.sharding import PartitionSpec as P

viscosity = 0.5
step_weight = 0.25
LANE = 128
PIECES = 2
in_hbm = pl.BlockSpec(memory_space=pltpu.HBM)
in_vmem = pl.BlockSpec(memory_space=pltpu.VMEM)


def hold(array):
    return pltpu.with_memory_space_constraint(array, pltpu.HBM)


def halves(value):
    high = value.astype(jnp.bfloat16)
    low = (value - high.astype(jnp.float32)).astype(jnp.bfloat16)
    return high, low


def product(left, right, contract):
    dims = ((contract[0:1], contract[1:2]), ((), ()))
    dot = functools.partial(
        lax.dot_general, dimension_numbers=dims, preferred_element_type=jnp.float32
    )
    return dot(left[0], right[0]) + (dot(left[0], right[1]) + dot(left[1], right[0]))


def pack_kernel(adj_ref, base_ref, after_ref, out_ref, held_ref, slab_ref, sem_ref, out_sem_ref):
    fields, planes = adj_ref.shape[1:3]
    chunks = out_ref.shape[0] // planes
    parts = out_sem_ref.shape[1]
    count = chunks // parts
    copies = []
    for z in range(planes):
        for field in range(fields + 1):
            source = adj_ref.at[0, field, z] if field < fields else base_ref.at[0, 1, z]
            copy = pltpu.make_async_copy(source, held_ref.at[z, field], sem_ref.at[z, field])
            copy.start()
            copies.append(copy)
    sends = []
    for z in range(planes):
        for copy in copies[z * (fields + 1) : (z + 1) * (fields + 1)]:
            copy.wait()
        for part in range(parts):
            for chunk in range(part * count, (part + 1) * count):
                slab_ref[z * chunks + chunk] = held_ref[z, :, :, pl.ds(chunk * LANE, LANE)]
            slabs = pl.ds(z * chunks + part * count, count)
            send = pltpu.make_async_copy(
                slab_ref.at[slabs], out_ref.at[slabs], out_sem_ref.at[z, part]
            )
            send.start()
            sends.append(send)
    for send in sends:
        send.wait()


def pack(adjoint, base_flow, after):
    _, fields, planes, rows, nx = adjoint.shape
    chunks = nx // LANE
    return pl.pallas_call(
        pack_kernel,
        in_specs=[in_hbm, in_hbm, in_hbm],
        out_specs=in_hbm,
        out_shape=pltpu.HBM((planes * chunks, fields + 1, rows, LANE), jnp.float32),
        scratch_shapes=[
            pltpu.VMEM((planes, fields + 1, rows, nx), jnp.float32),
            pltpu.VMEM((planes * chunks, fields + 1, rows, LANE), jnp.float32),
            pltpu.SemaphoreType.DMA((planes, fields + 1)),
            pltpu.SemaphoreType.DMA((planes, 4)),
        ],
        compiler_params=pltpu.CompilerParams(vmem_limit_bytes=4 * 2**20),
        name="pack_lines",
    )(hold(adjoint), hold(base_flow), hold(after))


def stream_kernel(turn, *refs):
    adj_ref, base_ref, first_ref, second_ref = refs[:4]
    extra = 4 * turn
    scratch = refs[len(refs) - 8 - extra :]
    field_ref, speed_ref, first, second, high_ref, low_ref, acc_ref, sem_ref = scratch[:8]
    outs = refs[len(refs) - 9 - extra - 2 * turn : len(refs) - 8 - extra]
    out_ref = outs[0]
    fields, planes, rows, nx = field_ref.shape
    blocks = nx // LANE
    lines = fields * planes * rows

    mine = lax.rem(lax.axis_index("col"), 2) == turn

    @pl.when(mine)
    def _():
        loads = [
            pltpu.make_async_copy(source, target, sem_ref.at[k])
            for k, (source, target) in enumerate(
                (
                    (adj_ref.at[0], field_ref),
                    (base_ref.at[0, 0], speed_ref),
                    (first_ref, first),
                    (second_ref, second),
                )
            )
        ]
        for load in loads:
            load.start()
        loads[0].wait()
        for q in range(blocks):
            block = field_ref[:, :, :, pl.ds(q * LANE, LANE)].reshape(lines, LANE)
            high, low = halves(block)
            for place in (q, q + blocks):
                if place < 2 * blocks - 1:
                    high_ref[pl.ds(place * lines, lines), :] = high
                    low_ref[pl.ds(place * lines, lines), :] = low
        acc_ref[...] = jnp.zeros_like(acc_ref)
        for load in loads[1:]:
            load.wait()

        @pl.loop(0, blocks // 2)
        def _(step):
            weights = jnp.concatenate(
                [
                    jnp.concatenate([ref[2 * step], ref[2 * step + 1]], axis=1)
                    for ref in (first, second)
                ],
                axis=0,
            )
            total = blocks * lines
            near = pl.ds(pl.multiple_of(step * (2 * lines), 2 * lines), total)
            far = pl.ds(pl.multiple_of(step * (2 * lines) + lines, lines), total)
            left = tuple(
                jnp.concatenate([ref[near, :], ref[far, :]], axis=1) for ref in (high_ref, low_ref)
            )
            acc_ref[...] += product(left, halves(weights), (1, 1))

        for p in range(blocks):
            lanes = pl.ds(p * LANE, LANE)
            x_first = acc_ref[pl.ds(p * lines, lines), pl.ds(0, LANE)]
            x_second = acc_ref[pl.ds(p * lines, lines), pl.ds(LANE, LANE)]
            x_first = x_first.reshape(fields, planes, rows, LANE)
            x_second = x_second.reshape(fields, planes, rows, LANE)
            rhs = viscosity * x_second + speed_ref[:, :, lanes][None] * x_first
            target = out_ref if turn == 0 else field_ref
            target[:, :, :, lanes] = field_ref[:, :, :, lanes] + step_weight * rhs
        if turn == 0:
            return
        copy = pltpu.make_async_copy(field_ref, out_ref, sem_ref.at[0])
        copy.start()
        copy.wait()
        if turn == 1:
            split_operators(refs[4:6], outs[1:], *scratch[8:])

    if turn == 0:

        @pl.when(jnp.logical_not(mine))
        def _():
            copy = pltpu.make_async_copy(refs[4], out_ref, sem_ref.at[0])
            copy.start()
            copy.wait()


def split_operators(wall_refs, out_refs, value_ref, whigh_ref, wlow_ref, sem_ref):
    loads = [
        pltpu.make_async_copy(ref, value_ref.at[k], sem_ref.at[k])
        for k, ref in enumerate(wall_refs)
    ]
    for load in loads:
        load.start()
    for which, load in enumerate(loads):
        load.wait()
        whigh_ref[which], wlow_ref[which] = halves(value_ref[which])
    stores = [
        pltpu.make_async_copy(ref, out, sem_ref.at[k])
        for k, (ref, out) in enumerate(zip((whigh_ref, wlow_ref), out_refs))
    ]
    for store in stores:
        store.start()
    for store in stores:
        store.wait()


def stream(turn, adjoint, base_flow, stream_first, stream_second, walls=(), before=None):
    _, fields, planes, rows, nx = adjoint.shape
    blocks = nx // LANE
    lines = fields * planes * rows
    operands = [adjoint, base_flow, stream_first, stream_second, *walls]
    shapes = [jax.ShapeDtypeStruct((fields, planes, rows, nx), jnp.float32)]
    scratch = []
    if turn == 1:
        both = (2, *walls[0].shape)
        shapes = [pltpu.HBM((fields, planes, rows, nx), jnp.float32)]
        shapes += [pltpu.HBM(both, jnp.bfloat16)] * 2
        scratch = [
            pltpu.VMEM(both, jnp.float32),
            pltpu.VMEM(both, jnp.bfloat16),
            pltpu.VMEM(both, jnp.bfloat16),
            pltpu.SemaphoreType.DMA((2,)),
        ]
    if before is not None:
        operands.append(before)
    return pl.pallas_call(
        functools.partial(stream_kernel, turn),
        in_specs=[in_hbm] * len(operands),
        out_specs=[in_hbm if turn == 1 else in_vmem] * len(shapes),
        out_shape=shapes,
        scratch_shapes=[
            pltpu.VMEM((fields, planes, rows, nx), jnp.float32),
            pltpu.VMEM((planes, rows, nx), jnp.float32),
            pltpu.VMEM(stream_first.shape, jnp.float32),
            pltpu.VMEM(stream_second.shape, jnp.float32),
            pltpu.VMEM(((2 * blocks - 1) * lines, LANE), jnp.bfloat16),
            pltpu.VMEM(((2 * blocks - 1) * lines, LANE), jnp.bfloat16),
            pltpu.VMEM((blocks * lines, 2 * LANE), jnp.float32),
            pltpu.SemaphoreType.DMA((4,)),
        ]
        + scratch,
        compiler_params=pltpu.CompilerParams(vmem_limit_bytes=28 * 2**20),
        cost_estimate=pl.CostEstimate(
            flops=6 * 2 * lines * nx * nx, bytes_accessed=8 * 2**20, transcendentals=0
        ),
        name="stream_sweep",
    )(*map(hold, operands))


def split_kernel(wall1_ref, wall2_ref, had1_ref, had2_ref, whigh_ref, wlow_ref, value_ref, sem_ref):
    late = lax.rem(lax.axis_index("col"), 2) == 1

    @pl.when(late)
    def _():
        loads = [
            pltpu.make_async_copy(source, target, sem_ref.at[k])
            for k, (source, target) in enumerate(((had1_ref, whigh_ref), (had2_ref, wlow_ref)))
        ]
        for load in loads:
            load.start()
        for load in loads:
            load.wait()

    @pl.when(jnp.logical_not(late))
    def _():
        loads = [
            pltpu.make_async_copy(ref, value_ref.at[k], sem_ref.at[k])
            for k, ref in enumerate((wall1_ref, wall2_ref))
        ]
        for load in loads:
            load.start()
        for which, load in enumerate(loads):
            load.wait()
            whigh_ref[which], wlow_ref[which] = halves(value_ref[which])


def split(wall_first, wall_second, whigh, wlow):
    return pl.pallas_call(
        split_kernel,
        in_specs=[in_hbm] * 4,
        out_specs=[in_vmem] * 2,
        out_shape=[jax.ShapeDtypeStruct(whigh.shape, jnp.bfloat16)] * 2,
        scratch_shapes=[pltpu.VMEM(whigh.shape, jnp.float32), pltpu.SemaphoreType.DMA((2,))],
        compiler_params=pltpu.CompilerParams(vmem_limit_bytes=8 * 2**20),
        cost_estimate=pl.CostEstimate(flops=2**21, bytes_accessed=4 * 2**20, transcendentals=0),
        name="split_wall",
    )(*map(hold, (wall_first, wall_second, whigh, wlow)))


def wall_kernel(lines_ref, whigh_ref, wlow_ref, out_ref, held_ref, sem_ref):
    chunks, slabs, rows, _ = lines_ref.shape
    fields = slabs - 1
    ny = chunks * rows
    parts = [halves(lines_ref[:, f].reshape(ny, LANE)) for f in range(fields)]
    values = jnp.concatenate([part[k] for k in range(2) for part in parts], axis=1)
    width = fields * LANE
    dot = functools.partial(jnp.dot, preferred_element_type=jnp.float32)
    pieces = sem_ref.shape[0]
    length, count = ny // pieces, chunks // pieces
    copies = []
    for piece in range(pieces):
        own, slab = pl.ds(piece * length, length), pl.ds(piece * count, count)
        weights = tuple(
            jnp.concatenate([ref[0, own, :], ref[1, own, :]], axis=0)
            for ref in (whigh_ref, wlow_ref)
        )
        both = dot(weights[0], values)
        both = both[:, :width] + (both[:, width:] + dot(weights[1], values[:, :width]))
        speed = lines_ref[slab, fields].reshape(length, LANE)
        for f in range(fields):
            lanes = slice(f * LANE, (f + 1) * LANE)
            rhs = step_weight * (
                viscosity * both[length:, lanes] + speed * both[:length, lanes]
            )
            held_ref[slab, f] = rhs.reshape(count, rows, LANE)
        copy = pltpu.make_async_copy(held_ref.at[slab], out_ref.at[slab], sem_ref.at[piece])
        copy.start()
        copies.append(copy)
    for copy in copies:
        copy.wait()


def wall(lines, whigh, wlow):
    chunks, slabs, rows, _ = lines.shape
    ny = chunks * rows
    shape = (chunks, slabs - 1, rows, LANE)
    return pl.pallas_call(
        wall_kernel,
        in_specs=[in_vmem, in_vmem, in_vmem],
        out_specs=in_hbm,
        out_shape=pltpu.HBM(shape, jnp.float32),
        scratch_shapes=[
            pltpu.VMEM(shape, jnp.float32),
            pltpu.SemaphoreType.DMA((PIECES,)),
        ],
        compiler_params=pltpu.CompilerParams(vmem_limit_bytes=12 * 2**20),
        cost_estimate=pl.CostEstimate(
            flops=6 * 2 * ny * ny * LANE * (slabs - 1), bytes_accessed=4 * 2**20, transcendentals=0
        ),
        name="wall_sweep",
    )(lines, whigh, wlow)


def update_kernel(stream_ref, wall_ref, *out_refs):
    fields, planes, rows, nx = stream_ref.shape
    chunks = nx // LANE
    for z in range(planes):
        for chunk in range(chunks):
            lanes = pl.ds(chunk * LANE, LANE)
            for field in range(fields):
                out_refs[z][field, :, lanes] = (
                    stream_ref[field, z, :, lanes] + wall_ref[z * chunks + chunk, field]
                )


def update(streamed, walled):
    fields, planes, rows, nx = streamed.shape
    return pl.pallas_call(
        update_kernel,
        in_specs=[in_vmem, in_vmem],
        out_specs=[in_vmem] * planes,
        out_shape=[jax.ShapeDtypeStruct((fields, rows, nx), jnp.float32)] * planes,
        compiler_params=pltpu.CompilerParams(vmem_limit_bytes=4 * 2**20),
        name="add_sweeps",
    )(streamed, walled)


def keep_kernel(planes, *refs):
    updated_refs, forcing_ref, out_ref = refs[:planes], refs[planes], refs[planes + 1]
    early_refs, sem_ref = refs[planes + 2 : -1], refs[-1]
    copies = [
        pltpu.make_async_copy(ref, out_ref.at[0, :, z], sem_ref.at[z])
        for z, ref in enumerate(updated_refs)
    ]
    for copy in copies:
        copy.start()
    for z, ref in enumerate(updated_refs):
        early_refs[z][...] = forcing_ref[:, z] * ref[...]
    for copy in copies:
        copy.wait()


def keep(updated, forcing):
    planes = len(updated)
    return pl.pallas_call(
        functools.partial(keep_kernel, planes),
        in_specs=[in_vmem] * (planes + 1),
        out_specs=[in_hbm] + [in_vmem] * planes,
        out_shape=[pltpu.HBM((1, *forcing.shape), jnp.float32)]
        + [jax.ShapeDtypeStruct(part.shape, jnp.float32) for part in updated],
        scratch_shapes=[pltpu.SemaphoreType.DMA((planes,))],
        compiler_params=pltpu.CompilerParams(vmem_limit_bytes=4 * 2**20),
        name="keep_updated",
    )(*updated, forcing)


def gradient_kernel(z, early_ref, forcing_ref, other_ref, *refs):
    out_ref, held_ref, sem_ref = refs[-3:]
    copies = []
    for field in range(forcing_ref.shape[0]):
        held_ref[field] = early_ref[field] + forcing_ref[field, z] * other_ref[field]
        copy = pltpu.make_async_copy(held_ref.at[field], out_ref.at[field, z], sem_ref.at[field])
        copy.start()
        copies.append(copy)
    for copy in copies:
        copy.wait()


def gradient(z, early, forcing, other, before):
    earlier = [] if before is None else [hold(before)]
    return pl.pallas_call(
        functools.partial(gradient_kernel, z),
        in_specs=[in_vmem] * 3 + [in_hbm] * len(earlier),
        out_specs=in_hbm,
        out_shape=pltpu.HBM(forcing.shape, jnp.float32),
        input_output_aliases={3: 0} if earlier else {},
        scratch_shapes=[
            pltpu.VMEM(early.shape, jnp.float32),
            pltpu.SemaphoreType.DMA(forcing.shape[:1]),
        ],
        compiler_params=pltpu.CompilerParams(vmem_limit_bytes=4 * 2**20),
        name="body_force",
    )(early, forcing, other, *earlier)


def local(adjoint, base_flow, stream_first, stream_second, wall_first, wall_second, forcing):
    operators = (stream_first, stream_second)
    walls = (wall_first, wall_second)
    streamed, whigh, wlow = stream(1, adjoint, base_flow, *operators, walls=walls)
    lines = lax.all_to_all(pack(adjoint, base_flow, streamed), "row", 0, 0)
    (streamed,) = stream(0, adjoint, base_flow, *operators, before=streamed)
    whigh, wlow = split(*walls, whigh, wlow)
    walled = lax.all_to_all(wall(lines, whigh, wlow), "row", 0, 0)
    updated = update(streamed, walled)
    others = [lax.ppermute(part, "ens", [(0, 1), (1, 0)]) for part in updated]
    kept, *early = keep(updated, forcing)
    result = None
    for z, (own, other) in enumerate(zip(early, others)):
        result = gradient(z, own, forcing, other, result)
    return kept, result


def solution(mesh):
    placed = (
        P("ens", None, "col", "row", None),
        P("ens", None, "col", "row", None),
        P(),
        P(),
        P(),
        P(),
        P(None, "col", "row", None),
    )
    return jax.shard_map(
        local,
        mesh=mesh,
        in_specs=placed,
        out_specs=(P("ens", None, "col", "row", None), P(None, "col", "row", None)),
        check_vma=False,
    )
```

```python
import functools

import jax
import jax.numpy as jnp
from jax import lax
from jax.experimental import pallas as pl
from jax.experimental.pallas import tpu as pltpu
from jax.sharding import PartitionSpec as P

viscosity = 0.5
step_weight = 0.25
LANE = 128
PIECES = 4
in_hbm = pl.BlockSpec(memory_space=pltpu.HBM)
in_vmem = pl.BlockSpec(memory_space=pltpu.VMEM)


def hold(array):
    return pltpu.with_memory_space_constraint(array, pltpu.HBM)


def halves(value):
    high = value.astype(jnp.bfloat16)
    low = (value - high.astype(jnp.float32)).astype(jnp.bfloat16)
    return high, low


def product(left, right, contract):
    dims = ((contract[0:1], contract[1:2]), ((), ()))
    dot = functools.partial(
        lax.dot_general, dimension_numbers=dims, preferred_element_type=jnp.float32
    )
    return dot(left[0], right[0]) + (dot(left[0], right[1]) + dot(left[1], right[0]))


def pack_kernel(adj_ref, base_ref, after_ref, out_ref, held_ref, slab_ref, sem_ref, out_sem_ref):
    fields, planes = adj_ref.shape[1:3]
    chunks = out_ref.shape[0] // planes
    parts = out_sem_ref.shape[1]
    count = chunks // parts
    copies = []
    for z in range(planes):
        for field in range(fields + 1):
            source = adj_ref.at[0, field, z] if field < fields else base_ref.at[0, 1, z]
            copy = pltpu.make_async_copy(source, held_ref.at[z, field], sem_ref.at[z, field])
            copy.start()
            copies.append(copy)
    sends = []
    for z in range(planes):
        for copy in copies[z * (fields + 1) : (z + 1) * (fields + 1)]:
            copy.wait()
        for part in range(parts):
            for chunk in range(part * count, (part + 1) * count):
                slab_ref[z * chunks + chunk] = held_ref[z, :, :, pl.ds(chunk * LANE, LANE)]
            slabs = pl.ds(z * chunks + part * count, count)
            send = pltpu.make_async_copy(
                slab_ref.at[slabs], out_ref.at[slabs], out_sem_ref.at[z, part]
            )
            send.start()
            sends.append(send)
    for send in sends:
        send.wait()


def pack(adjoint, base_flow, after):
    _, fields, planes, rows, nx = adjoint.shape
    chunks = nx // LANE
    return pl.pallas_call(
        pack_kernel,
        in_specs=[in_hbm, in_hbm, in_hbm],
        out_specs=in_hbm,
        out_shape=pltpu.HBM((planes * chunks, fields + 1, rows, LANE), jnp.float32),
        scratch_shapes=[
            pltpu.VMEM((planes, fields + 1, rows, nx), jnp.float32),
            pltpu.VMEM((planes * chunks, fields + 1, rows, LANE), jnp.float32),
            pltpu.SemaphoreType.DMA((planes, fields + 1)),
            pltpu.SemaphoreType.DMA((planes, 4)),
        ],
        compiler_params=pltpu.CompilerParams(vmem_limit_bytes=4 * 2**20),
        name="pack_lines",
    )(hold(adjoint), hold(base_flow), hold(after))


def stream_kernel(turn, *refs):
    adj_ref, base_ref, first_ref, second_ref = refs[:4]
    extra = 4 * turn
    scratch = refs[len(refs) - 8 - extra :]
    field_ref, speed_ref, first, second, high_ref, low_ref, acc_ref, sem_ref = scratch[:8]
    outs = refs[len(refs) - 9 - extra - 2 * turn : len(refs) - 8 - extra]
    out_ref = outs[0]
    fields, planes, rows, nx = field_ref.shape
    blocks = nx // LANE
    lines = fields * planes * rows

    mine = lax.rem(lax.axis_index("col"), 2) == turn

    @pl.when(mine)
    def _():
        loads = [
            pltpu.make_async_copy(source, target, sem_ref.at[k])
            for k, (source, target) in enumerate(
                (
                    (adj_ref.at[0], field_ref),
                    (base_ref.at[0, 0], speed_ref),
                    (first_ref, first),
                    (second_ref, second),
                )
            )
        ]
        for load in loads:
            load.start()
        loads[0].wait()
        for q in range(blocks):
            block = field_ref[:, :, :, pl.ds(q * LANE, LANE)].reshape(lines, LANE)
            high, low = halves(block)
            for place in (q, q + blocks):
                if place < 2 * blocks - 1:
                    high_ref[pl.ds(place * lines, lines), :] = high
                    low_ref[pl.ds(place * lines, lines), :] = low
        acc_ref[...] = jnp.zeros_like(acc_ref)
        for load in loads[1:]:
            load.wait()

        @pl.loop(0, blocks // 2)
        def _(step):
            weights = jnp.concatenate(
                [
                    jnp.concatenate([ref[2 * step], ref[2 * step + 1]], axis=1)
                    for ref in (first, second)
                ],
                axis=0,
            )
            total = blocks * lines
            near = pl.ds(pl.multiple_of(step * (2 * lines), 2 * lines), total)
            far = pl.ds(pl.multiple_of(step * (2 * lines) + lines, lines), total)
            left = tuple(
                jnp.concatenate([ref[near, :], ref[far, :]], axis=1) for ref in (high_ref, low_ref)
            )
            acc_ref[...] += product(left, halves(weights), (1, 1))

        for p in range(blocks):
            lanes = pl.ds(p * LANE, LANE)
            x_first = acc_ref[pl.ds(p * lines, lines), pl.ds(0, LANE)]
            x_second = acc_ref[pl.ds(p * lines, lines), pl.ds(LANE, LANE)]
            x_first = x_first.reshape(fields, planes, rows, LANE)
            x_second = x_second.reshape(fields, planes, rows, LANE)
            rhs = viscosity * x_second + speed_ref[:, :, lanes][None] * x_first
            target = out_ref if turn == 0 else field_ref
            target[:, :, :, lanes] = field_ref[:, :, :, lanes] + step_weight * rhs
        if turn == 0:
            return
        copy = pltpu.make_async_copy(field_ref, out_ref, sem_ref.at[0])
        copy.start()
        copy.wait()
        if turn == 1:
            split_operators(refs[4:6], outs[1:], *scratch[8:])

    if turn == 0:

        @pl.when(jnp.logical_not(mine))
        def _():
            copy = pltpu.make_async_copy(refs[4], out_ref, sem_ref.at[0])
            copy.start()
            copy.wait()


def split_operators(wall_refs, out_refs, value_ref, whigh_ref, wlow_ref, sem_ref):
    loads = [
        pltpu.make_async_copy(ref, value_ref.at[k], sem_ref.at[k])
        for k, ref in enumerate(wall_refs)
    ]
    for load in loads:
        load.start()
    for which, load in enumerate(loads):
        load.wait()
        whigh_ref[which], wlow_ref[which] = halves(value_ref[which])
    stores = [
        pltpu.make_async_copy(ref, out, sem_ref.at[k])
        for k, (ref, out) in enumerate(zip((whigh_ref, wlow_ref), out_refs))
    ]
    for store in stores:
        store.start()
        store.wait()


def stream(turn, adjoint, base_flow, stream_first, stream_second, walls=(), before=None):
    _, fields, planes, rows, nx = adjoint.shape
    blocks = nx // LANE
    lines = fields * planes * rows
    operands = [adjoint, base_flow, stream_first, stream_second, *walls]
    shapes = [jax.ShapeDtypeStruct((fields, planes, rows, nx), jnp.float32)]
    scratch = []
    if turn == 1:
        both = (2, *walls[0].shape)
        shapes = [pltpu.HBM((fields, planes, rows, nx), jnp.float32)]
        shapes += [pltpu.HBM(both, jnp.bfloat16)] * 2
        scratch = [
            pltpu.VMEM(both, jnp.float32),
            pltpu.VMEM(both, jnp.bfloat16),
            pltpu.VMEM(both, jnp.bfloat16),
            pltpu.SemaphoreType.DMA((2,)),
        ]
    if before is not None:
        operands.append(before)
    return pl.pallas_call(
        functools.partial(stream_kernel, turn),
        in_specs=[in_hbm] * len(operands),
        out_specs=[in_hbm if turn == 1 else in_vmem] * len(shapes),
        out_shape=shapes,
        scratch_shapes=[
            pltpu.VMEM((fields, planes, rows, nx), jnp.float32),
            pltpu.VMEM((planes, rows, nx), jnp.float32),
            pltpu.VMEM(stream_first.shape, jnp.float32),
            pltpu.VMEM(stream_second.shape, jnp.float32),
            pltpu.VMEM(((2 * blocks - 1) * lines, LANE), jnp.bfloat16),
            pltpu.VMEM(((2 * blocks - 1) * lines, LANE), jnp.bfloat16),
            pltpu.VMEM((blocks * lines, 2 * LANE), jnp.float32),
            pltpu.SemaphoreType.DMA((4,)),
        ]
        + scratch,
        compiler_params=pltpu.CompilerParams(vmem_limit_bytes=28 * 2**20),
        cost_estimate=pl.CostEstimate(
            flops=6 * 2 * lines * nx * nx, bytes_accessed=8 * 2**20, transcendentals=0
        ),
        name="stream_sweep",
    )(*map(hold, operands))


def split_kernel(wall1_ref, wall2_ref, had1_ref, had2_ref, whigh_ref, wlow_ref, value_ref, sem_ref):
    late = lax.rem(lax.axis_index("col"), 2) == 1

    @pl.when(late)
    def _():
        loads = [
            pltpu.make_async_copy(source, target, sem_ref.at[k])
            for k, (source, target) in enumerate(((had1_ref, whigh_ref), (had2_ref, wlow_ref)))
        ]
        for load in loads:
            load.start()
        for load in loads:
            load.wait()

    @pl.when(jnp.logical_not(late))
    def _():
        loads = [
            pltpu.make_async_copy(ref, value_ref.at[k], sem_ref.at[k])
            for k, ref in enumerate((wall1_ref, wall2_ref))
        ]
        for load in loads:
            load.start()
        for which, load in enumerate(loads):
            load.wait()
            whigh_ref[which], wlow_ref[which] = halves(value_ref[which])


def split(wall_first, wall_second, whigh, wlow):
    return pl.pallas_call(
        split_kernel,
        in_specs=[in_hbm] * 4,
        out_specs=[in_vmem] * 2,
        out_shape=[jax.ShapeDtypeStruct(whigh.shape, jnp.bfloat16)] * 2,
        scratch_shapes=[pltpu.VMEM(whigh.shape, jnp.float32), pltpu.SemaphoreType.DMA((2,))],
        compiler_params=pltpu.CompilerParams(vmem_limit_bytes=8 * 2**20),
        cost_estimate=pl.CostEstimate(flops=2**21, bytes_accessed=4 * 2**20, transcendentals=0),
        name="split_wall",
    )(*map(hold, (wall_first, wall_second, whigh, wlow)))


def wall_kernel(lines_ref, whigh_ref, wlow_ref, out_ref, held_ref, sem_ref):
    chunks, slabs, rows, _ = lines_ref.shape
    fields = slabs - 1
    ny = chunks * rows
    parts = [halves(lines_ref[:, f].reshape(ny, LANE)) for f in range(fields)]
    values = jnp.concatenate([part[k] for k in range(2) for part in parts], axis=1)
    width = fields * LANE
    dot = functools.partial(jnp.dot, preferred_element_type=jnp.float32)
    pieces = sem_ref.shape[0]
    length, count = ny // pieces, chunks // pieces
    copies = []
    for piece in range(pieces):
        own, slab = pl.ds(piece * length, length), pl.ds(piece * count, count)
        weights = tuple(
            jnp.concatenate([ref[0, own, :], ref[1, own, :]], axis=0)
            for ref in (whigh_ref, wlow_ref)
        )
        both = dot(weights[0], values)
        both = both[:, :width] + (both[:, width:] + dot(weights[1], values[:, :width]))
        speed = lines_ref[slab, fields].reshape(length, LANE)
        for f in range(fields):
            lanes = slice(f * LANE, (f + 1) * LANE)
            rhs = step_weight * (
                viscosity * both[length:, lanes] + speed * both[:length, lanes]
            )
            held_ref[slab, f] = rhs.reshape(count, rows, LANE)
        copy = pltpu.make_async_copy(held_ref.at[slab], out_ref.at[slab], sem_ref.at[piece])
        copy.start()
        copies.append(copy)
    for copy in copies:
        copy.wait()


def wall(lines, whigh, wlow):
    chunks, slabs, rows, _ = lines.shape
    ny = chunks * rows
    shape = (chunks, slabs - 1, rows, LANE)
    return pl.pallas_call(
        wall_kernel,
        in_specs=[in_vmem, in_vmem, in_vmem],
        out_specs=in_hbm,
        out_shape=pltpu.HBM(shape, jnp.float32),
        scratch_shapes=[
            pltpu.VMEM(shape, jnp.float32),
            pltpu.SemaphoreType.DMA((PIECES,)),
        ],
        compiler_params=pltpu.CompilerParams(vmem_limit_bytes=12 * 2**20),
        cost_estimate=pl.CostEstimate(
            flops=6 * 2 * ny * ny * LANE * (slabs - 1), bytes_accessed=4 * 2**20, transcendentals=0
        ),
        name="wall_sweep",
    )(lines, whigh, wlow)


def update_kernel(stream_ref, wall_ref, *out_refs):
    fields, planes, rows, nx = stream_ref.shape
    chunks = nx // LANE
    for z in range(planes):
        for chunk in range(chunks):
            lanes = pl.ds(chunk * LANE, LANE)
            for field in range(fields):
                out_refs[z][field, :, lanes] = (
                    stream_ref[field, z, :, lanes] + wall_ref[z * chunks + chunk, field]
                )


def update(streamed, walled):
    fields, planes, rows, nx = streamed.shape
    return pl.pallas_call(
        update_kernel,
        in_specs=[in_vmem, in_vmem],
        out_specs=[in_vmem] * planes,
        out_shape=[jax.ShapeDtypeStruct((fields, rows, nx), jnp.float32)] * planes,
        compiler_params=pltpu.CompilerParams(vmem_limit_bytes=4 * 2**20),
        name="add_sweeps",
    )(streamed, walled)


def keep_kernel(planes, *refs):
    updated_refs, forcing_ref, out_ref = refs[:planes], refs[planes], refs[planes + 1]
    early_refs, sem_ref = refs[planes + 2 : -1], refs[-1]
    copies = [
        pltpu.make_async_copy(ref, out_ref.at[0, :, z], sem_ref.at[z])
        for z, ref in enumerate(updated_refs)
    ]
    for copy in copies:
        copy.start()
    for z, ref in enumerate(updated_refs):
        early_refs[z][...] = forcing_ref[:, z] * ref[...]
    for copy in copies:
        copy.wait()


def keep(updated, forcing):
    planes = len(updated)
    return pl.pallas_call(
        functools.partial(keep_kernel, planes),
        in_specs=[in_vmem] * (planes + 1),
        out_specs=[in_hbm] + [in_vmem] * planes,
        out_shape=[pltpu.HBM((1, *forcing.shape), jnp.float32)]
        + [jax.ShapeDtypeStruct(part.shape, jnp.float32) for part in updated],
        scratch_shapes=[pltpu.SemaphoreType.DMA((planes,))],
        compiler_params=pltpu.CompilerParams(vmem_limit_bytes=4 * 2**20),
        name="keep_updated",
    )(*updated, forcing)


def gradient_kernel(z, early_ref, forcing_ref, other_ref, *refs):
    out_ref, held_ref, sem_ref = refs[-3:]
    copies = []
    for field in range(forcing_ref.shape[0]):
        held_ref[field] = early_ref[field] + forcing_ref[field, z] * other_ref[field]
        copy = pltpu.make_async_copy(held_ref.at[field], out_ref.at[field, z], sem_ref.at[field])
        copy.start()
        copies.append(copy)
    for copy in copies:
        copy.wait()


def gradient(z, early, forcing, other, before):
    earlier = [] if before is None else [hold(before)]
    return pl.pallas_call(
        functools.partial(gradient_kernel, z),
        in_specs=[in_vmem] * 3 + [in_hbm] * len(earlier),
        out_specs=in_hbm,
        out_shape=pltpu.HBM(forcing.shape, jnp.float32),
        input_output_aliases={3: 0} if earlier else {},
        scratch_shapes=[
            pltpu.VMEM(early.shape, jnp.float32),
            pltpu.SemaphoreType.DMA(forcing.shape[:1]),
        ],
        compiler_params=pltpu.CompilerParams(vmem_limit_bytes=4 * 2**20),
        name="body_force",
    )(early, forcing, other, *earlier)


def local(adjoint, base_flow, stream_first, stream_second, wall_first, wall_second, forcing):
    operators = (stream_first, stream_second)
    walls = (wall_first, wall_second)
    streamed, whigh, wlow = stream(1, adjoint, base_flow, *operators, walls=walls)
    lines = lax.all_to_all(pack(adjoint, base_flow, streamed), "row", 0, 0)
    (streamed,) = stream(0, adjoint, base_flow, *operators, before=streamed)
    whigh, wlow = split(*walls, whigh, wlow)
    walled = lax.all_to_all(wall(lines, whigh, wlow), "row", 0, 0)
    updated = update(streamed, walled)
    others = [lax.ppermute(part, "ens", [(0, 1), (1, 0)]) for part in updated]
    kept, *early = keep(updated, forcing)
    result = None
    for z, (own, other) in enumerate(zip(early, others)):
        result = gradient(z, own, forcing, other, result)
    return kept, result


def solution(mesh):
    placed = (
        P("ens", None, "col", "row", None),
        P("ens", None, "col", "row", None),
        P(),
        P(),
        P(),
        P(),
        P(None, "col", "row", None),
    )
    return jax.shard_map(
        local,
        mesh=mesh,
        in_specs=placed,
        out_specs=(P("ens", None, "col", "row", None), P(None, "col", "row", None)),
        check_vma=False,
    )
```
